32 devices in a mesh: ind: 8 (over y, x, core), snp: 4 (over z).
Axes of the slice: x: 2, y: 2, z: 4, core: 2. Of those that a mesh axis runs over, the one named last changes fastest.
Arguments:
- genotypes: int32 [8192, 4096], P('ind', 'snp'), may hold values from 0 to 2, as said below
- ancestry: float32 [16, 8192], P(None, ('ind', 'snp')), may hold values from 0 to 1, as said below
- freqs: float32 [16, 4096], P(None, ('snp', 'ind')), may hold values from 0.05 to 0.95
Outputs:
- ancestry_new: float32 [16, 8192], P(None, ('ind', 'snp'))
- freqs_new: float32 [16, 4096], P(None, ('snp', 'ind'))
The draws below stay inside these ranges and needn't reach their ends.
Inputs may be any that keep to these rules, and one draw needn't show every extreme that they name: `genotypes`: each count is 0, 1 or 2. `ancestry`: all entries are positive and each column sums to one.
All inputs are finite; a program needn't handle non-finite values.
Results may differ from the reference program's by a relative error of at most 0.0001.
Values sent between devices are 32-bit elements; how exact they have to be, the bound alone decides.
No kernel may reach another device: no remote copies, remote signals or barrier semaphores. Data moves between devices by JAX's collectives and lax.ppermute only.
A program may use at most 64 MiB of HBM per device.

```python
import jax
import jax.numpy as jnp
from jax import lax

IND_DEV = 1024
ANCESTRIES = 16
ITERS = 4
POPS = 8
INDIVIDUALS = 8192
SNPS = 4096


def draw_genotypes(key, part):
    key = jax.random.fold_in(key, 11)
    key_table, key_first, key_second = jax.random.split(key, 3)
    groups = jnp.arange(INDIVIDUALS, dtype=jnp.int32) * POPS // INDIVIDUALS
    table = jax.random.randint(key_table, (POPS, SNPS), 1, 16, dtype=jnp.int32)
    levels = jnp.take(table, groups, axis=0)
    first = jax.random.randint(key_first, (INDIVIDUALS, SNPS), 0, 16, dtype=jnp.int32)
    second = jax.random.randint(key_second, (INDIVIDUALS, SNPS), 0, 16, dtype=jnp.int32)
    return (first < levels).astype(jnp.int32) + (second < levels).astype(jnp.int32)


def draw_ancestry(key, part):
    key = jax.random.fold_in(key, 23)
    logs = jax.random.uniform(key, (ANCESTRIES, INDIVIDUALS), jnp.float32, -2.3, 0.0)
    weights = jnp.exp(logs)
    return weights / jnp.sum(weights, axis=0, keepdims=True)


def shard_levels(key, extent, cuts, low, largest):
    loudness = 1.0
    for axis_at, shards_of in cuts:
        steps = jax.random.uniform(jax.random.fold_in(jax.random.fold_in(key, 6), axis_at), (shards_of,), jnp.float32, low / len(cuts), largest / len(cuts))
        loudness = loudness * jnp.repeat(jnp.exp(steps), extent[axis_at] // shards_of).reshape((-1,) + (1,) * (len(extent) - 1 - axis_at))
    return loudness


def setup_inputs(seed: int = 0) -> dict:
    streams_of = jax.random.split(jax.random.key(seed), 4)
    return {
        "genotypes": draw_genotypes(jax.random.fold_in(streams_of[3], 71), 0),
        "ancestry": draw_ancestry(jax.random.fold_in(streams_of[3], 71), 0),
        "freqs": jnp.clip(0.05 + 0.9 * jax.random.uniform(streams_of[2], (ANCESTRIES, SNPS), jnp.float32) ** shard_levels(streams_of[2], (ANCESTRIES, SNPS), ((1, 32),), -0.2, 0.2), 0.05, 0.95),
    }


def reference(genotypes, ancestry, freqs):
    total_rows = genotypes.shape[0]
    total_snps = genotypes.shape[1]
    nblocks = total_rows // IND_DEV
    g_blocks = genotypes.reshape(nblocks, IND_DEV, total_snps)
    for step in range(ITERS):
        q_blocks = ancestry.reshape(ANCESTRIES, nblocks, IND_DEV).transpose(1, 0, 2)
        current = freqs

        def visit(carry, item):
            g_int, q_block = item
            g_val = g_int.astype(jnp.float32)
            expected = lax.dot_general(q_block, current, (((0,), (0,)), ((), ())), precision=lax.Precision.HIGHEST)
            ratio_one = g_val / expected
            ratio_two = (2.0 - g_val) / (1.0 - expected)
            q_sum = lax.dot_general(current, ratio_one - ratio_two, (((1,), (1,)), ((), ())), precision=lax.Precision.HIGHEST)
            q_sum = q_sum + jnp.sum(ratio_two, axis=1)[None, :]
            p_one = jnp.dot(q_block, ratio_one, precision=lax.Precision.HIGHEST)
            p_two = jnp.dot(q_block, ratio_two, precision=lax.Precision.HIGHEST)
            return (carry[0] + p_one, carry[1] + p_two), q_sum

        zeros = jnp.zeros((ANCESTRIES, total_snps), jnp.float32)
        (p_one, p_two), q_sums = lax.scan(visit, (zeros, zeros), (g_blocks, q_blocks))
        q_sum = q_sums.transpose(1, 0, 2).reshape(ANCESTRIES, total_rows)
        ancestry = ancestry * q_sum / (2.0 * total_snps)
        freqs = current * p_one / (current * p_one + (1.0 - current) * p_two)
    return ancestry, freqs
```

```python
import functools

import jax
import jax.numpy as jnp
from jax import lax
from jax.experimental import pallas as pl
from jax.experimental.pallas import tpu as pltpu
from jax.sharding import PartitionSpec as P

ITERS = 4
AXES = ("ind", "snp")


def split3(x):
    one = x.astype(jnp.bfloat16)
    rest = x - one.astype(jnp.float32)
    two = rest.astype(jnp.bfloat16)
    three = (rest - two.astype(jnp.float32)).astype(jnp.bfloat16)
    return one, two, three


def fold3(x):
    k = x.shape[0] // 3
    return x[:k] + x[k : 2 * k] + x[2 * k :]


def em_kernel(first, rows, snps_all, core_ref, g_ref, q_ref, keep_ref, got_ref, mine_ref, send_ref, q_out, p_out, qs_ref, ql_ref, ps_ref, pr_ref, acc_ref):
    core = core_ref[0]
    keep, got = keep_ref[...], got_ref[...]
    p = jnp.where(core == 0, keep, got)
    a_sum = jnp.where(core == 0, got, keep)
    if first:
        q = a_sum
    else:
        q_old = q_ref[...]
        rest = 2.0 * snps_all - jnp.sum(q_old * a_sum, axis=0, keepdims=True)
        q = q_old * (a_sum + rest) * (1.0 / (2.0 * snps_all))
    q_out[...] = q
    p_out[...] = p
    k = q.shape[0]
    q1, q2, q3 = split3(q)
    p1, p2, p3 = split3(p)
    qs_ref[...] = jnp.concatenate([q1, q2, q3], axis=0)
    ps_ref[...] = jnp.concatenate([p1, p2, p3], axis=0)
    ql_ref[...] = jnp.concatenate([q1, q2, q1, q2, q3, q1], axis=0).T
    pr_ref[...] = jnp.concatenate([p1, p1, p2, p2, p1, p3], axis=0)
    acc_ref[...] = jnp.zeros_like(acc_ref)
    qsum_ref, other_ref = (send_ref, mine_ref)

    def block(b, _):
        at = pl.ds(pl.multiple_of(b * rows, rows), rows)
        e = jnp.dot(ql_ref[at, :], pr_ref[...], preferred_element_type=jnp.float32)
        g = g_ref[at, :].astype(jnp.float32)
        d = e * (1.0 - e)
        inv = pl.reciprocal(d, approx=True)
        inv = inv * (2.0 - d * inv)
        diff = (g - 2.0 * e) * inv
        two = ((2.0 - g) * e) * inv
        dh = diff.astype(jnp.bfloat16)
        dl = (diff - dh.astype(jnp.float32)).astype(jnp.bfloat16)
        th = two.astype(jnp.bfloat16)
        tl = (two - th.astype(jnp.float32)).astype(jnp.bfloat16)
        nt = (((1,), (1,)), ((), ()))
        a = lax.dot_general(ps_ref[...], dh, nt, preferred_element_type=jnp.float32)
        a = a + lax.dot_general(ps_ref[...], dl, nt, preferred_element_type=jnp.float32)
        a = fold3(a)
        mine_ref[k:, at] = a
        qb = qs_ref[:, at]
        pd = jnp.dot(qb, dh, preferred_element_type=jnp.float32) + jnp.dot(qb, dl, preferred_element_type=jnp.float32)
        pt = jnp.dot(qb, th, preferred_element_type=jnp.float32) + jnp.dot(qb, tl, preferred_element_type=jnp.float32)
        pt = fold3(pt)
        acc_ref[:k] += fold3(pd) + pt
        acc_ref[k:] += pt
        return 0

    lax.fori_loop(0, g_ref.shape[0] // rows, block, 0)
    a = mine_ref[k:, :]
    acc = acc_ref[...]

    @pl.when(core == 0)
    def _():
        send_ref[:k] = a
        send_ref[k:] = jnp.zeros_like(a)
        mine_ref[...] = acc

    @pl.when(core == 1)
    def _():
        send_ref[...] = acc
        mine_ref[:k] = jnp.zeros_like(a)


def em_step(first, snps_all, core, g, q, keep, got):
    individuals, snps = g.shape
    k = q.shape[0]
    f32, bf16 = jnp.float32, jnp.bfloat16
    vmem = pl.BlockSpec(memory_space=pltpu.VMEM)
    return pl.pallas_call(
        functools.partial(em_kernel, first, 256, snps_all),
        out_shape=(
            jax.ShapeDtypeStruct((2 * k, snps), f32),
            jax.ShapeDtypeStruct((2 * k, snps), f32),
            jax.ShapeDtypeStruct((k, individuals), f32),
            jax.ShapeDtypeStruct((k, snps), f32),
        ),
        in_specs=[pl.BlockSpec(memory_space=pltpu.SMEM)] + [vmem] * 4,
        out_specs=(vmem,) * 4,
        scratch_shapes=[
            pltpu.VMEM((3 * k, individuals), bf16),
            pltpu.VMEM((individuals, 6 * k), bf16),
            pltpu.VMEM((3 * k, snps), bf16),
            pltpu.VMEM((6 * k, snps), bf16),
            pltpu.VMEM((2 * k, snps), f32),
        ],
        compiler_params=pltpu.CompilerParams(vmem_limit_bytes=32 * 1024 * 1024),
        cost_estimate=pl.CostEstimate(flops=2 * 20 * k * individuals * snps, bytes_accessed=4 * individuals * snps, transcendentals=individuals * snps),
    )(core, g, q, keep, got)


def swap_cores(x, n_ind):
    return lax.ppermute(x, "ind", [(i, i ^ 1) for i in range(n_ind)])


def sum_groups(buf, n_ind, n_snp):
    n_chip = n_ind // 2
    base = 1
    while base < max(n_chip, n_snp):
        parts = []
        for m in (3, 2, 1):
            mask = m * base
            pairs = []
            for i in range(n_ind):
                for s in range(n_snp):
                    if i % 2 == 0 and mask < n_chip:
                        pairs.append((i * n_snp + s, (i ^ (2 * mask)) * n_snp + s))
                    if i % 2 == 1 and mask < n_snp:
                        pairs.append((i * n_snp + s, i * n_snp + (s ^ mask)))
            if pairs:
                parts.append(lax.ppermute(buf, AXES, pairs))
        for part in parts:
            buf = buf + part
        base *= 4
    return buf


def place(shard, index, count):
    width = shard.shape[1]
    full = jnp.zeros((shard.shape[0], width * count), shard.dtype)
    return lax.dynamic_update_slice_in_dim(full, shard, index * width, axis=1)


def body(genotypes, ancestry, freqs):
    n_ind, n_snp = lax.axis_size("ind"), lax.axis_size("snp")
    ind, snp = lax.axis_index("ind"), lax.axis_index("snp")
    core = ind % 2
    first_core = core == 0
    k = ancestry.shape[0]
    snps_all = genotypes.shape[1] * n_snp
    core_id = core.reshape(1).astype(jnp.int32)

    q_at = place(ancestry, snp, n_snp)
    p_at = place(freqs, ind, n_ind)
    none = jnp.zeros_like(q_at)
    mine = jnp.concatenate([jnp.where(first_core, p_at, none), jnp.where(first_core, none, q_at)])
    send = jnp.concatenate([jnp.where(first_core, q_at, p_at), none])
    q = none
    for step in range(ITERS + 1):
        buf = mine + swap_cores(send, n_ind)
        buf = sum_groups(buf, n_ind, n_snp)
        if step == 0:
            p_new = buf[:k]
        else:
            up = p * buf[:k]
            p_new = up / (up + (1.0 - p) * buf[k:])
        keep = jnp.where(first_core, p_new, buf[k:])
        got = swap_cores(jnp.where(first_core, p_new, buf[:k]), n_ind)
        if step < ITERS:
            mine, send, q, p = em_step(step == 0, snps_all, core_id, genotypes, q, keep, got)
    p = jnp.where(first_core, keep, got)
    a_sum = jnp.where(first_core, got, keep)
    rest = 2.0 * snps_all - jnp.sum(q * a_sum, axis=0, keepdims=True)
    q = q * (a_sum + rest) * (1.0 / (2.0 * snps_all))
    q_own = lax.dynamic_slice_in_dim(q, snp * ancestry.shape[1], ancestry.shape[1], axis=1)
    p_own = lax.dynamic_slice_in_dim(p, ind * freqs.shape[1], freqs.shape[1], axis=1)
    return (q_own, p_own)


def solution(mesh):
    in_specs = (P("ind", "snp"), P(None, ("ind", "snp")), P(None, ("snp", "ind")))
    out_specs = (P(None, ("ind", "snp")), P(None, ("snp", "ind")))
    return jax.shard_map(body, mesh=mesh, in_specs=in_specs, out_specs=out_specs, check_vma=False)
```

```python
import functools

import jax
import jax.numpy as jnp
from jax import lax
from jax.experimental import pallas as pl
from jax.experimental.pallas import tpu as pltpu
from jax.sharding import PartitionSpec as P

ITERS = 4
AXES = ("ind", "snp")
ROWS = 256
COLS = 256
NT = (((1,), (1,)), ((), ()))
SMEM = pl.BlockSpec(memory_space=pltpu.SMEM)
VMEM = pl.BlockSpec(memory_space=pltpu.VMEM)
HBM = pl.BlockSpec(memory_space=pltpu.HBM)


def split3(x):
    one = x.astype(jnp.bfloat16)
    rest = x - one.astype(jnp.float32)
    two = rest.astype(jnp.bfloat16)
    three = (rest - two.astype(jnp.float32)).astype(jnp.bfloat16)
    return one, two, three


def split2(x):
    one = x.astype(jnp.bfloat16)
    return one, (x - one.astype(jnp.float32)).astype(jnp.bfloat16)


def fold3(x):
    k = x.shape[0] // 3
    return x[:k] + x[k : 2 * k] + x[2 * k :]


def mxu(a, b, dims=(((1,), (0,)), ((), ()))):
    return lax.dot_general(a, b, dims, preferred_element_type=jnp.float32)


def new_ancestry(q, a_sum, snps_all):
    rest = snps_all - jnp.sum(q * a_sum, axis=0, keepdims=True)
    return q * (a_sum + rest) * (1.0 / snps_all)


def load_kernel(g_hbm, half_ref, buf, sems):
    n = buf.shape[0]
    rows = buf.shape[1]
    copies = [pltpu.make_async_copy(g_hbm.at[pl.ds(b * rows, rows)], buf.at[b], sems.at[b]) for b in range(n)]
    for copy in copies:
        copy.start()
    for b in range(n):
        copies[b].wait()
        half_ref[pl.ds(b * rows, rows), :] = 0.5 * buf[b].astype(jnp.float32)


def load_counts(genotypes):
    individuals, snps = genotypes.shape
    rows = 128
    n = individuals // rows
    return pl.pallas_call(
        load_kernel,
        out_shape=jax.ShapeDtypeStruct((individuals, snps), jnp.float32),
        in_specs=[HBM],
        out_specs=VMEM,
        scratch_shapes=[pltpu.VMEM((n, rows, snps), jnp.int32), pltpu.SemaphoreType.DMA((n,))],
        compiler_params=pltpu.CompilerParams(vmem_limit_bytes=16 * 1024 * 1024),
        cost_estimate=pl.CostEstimate(flops=individuals * snps, bytes_accessed=4 * individuals * snps, transcendentals=0),
    )(genotypes)


def em_kernel(first, snps_all, core_ref, g_ref, q_ref, keep_ref, got_ref, mine_ref, send_ref, q_out, p_out, qs_ref, ql_ref, ps_ref, pr_ref, dh_ref, dl_ref, th_ref, tl_ref):
    core = core_ref[0]
    keep, got = keep_ref[...], got_ref[...]
    p = jnp.where(core == 0, keep, got)
    a_sum = jnp.where(core == 0, got, keep)
    q = a_sum if first else new_ancestry(q_ref[...], a_sum, snps_all)
    q_out[...] = q
    p_out[...] = p
    k = q.shape[0]
    individuals, snps = g_ref.shape
    q1, q2, q3 = split3(q)
    p1, p2, p3 = split3(p)
    qs_ref[...] = jnp.concatenate([q1, q2, q3], axis=0)
    ps_ref[...] = jnp.concatenate([p1, p2, p3], axis=0)
    ql_ref[...] = jnp.concatenate([q1, q2, q1, q2, q3, q1], axis=0).T
    pr_ref[...] = jnp.concatenate([p1, p1, p2, p2, p1, p3], axis=0)

    def ratios(b):
        at = slice(b * ROWS, (b + 1) * ROWS)
        slot = b % 2
        for c in range(0, snps, COLS):
            to = slice(c, c + COLS)
            e = mxu(ql_ref[at, :], pr_ref[:, to])
            half = g_ref[at, to]
            d = e * (1.0 - e)
            inv = pltpu.reciprocal(d, approx=True)
            inv = inv * (2.0 - d * inv)
            diff = (half - e) * inv
            two = ((1.0 - half) * e) * inv
            dh_ref[slot, :, to], dl_ref[slot, :, to] = split2(diff)
            th_ref[slot, :, to], tl_ref[slot, :, to] = split2(two)

    pd = pt = 0.0
    blocks = individuals // ROWS
    for b in range(blocks + 1):
        if b < blocks:
            ratios(b)
        if b > 0:
            at = slice((b - 1) * ROWS, b * ROWS)
            slot = (b - 1) % 2
            dh, dl, th, tl = dh_ref[slot], dl_ref[slot], th_ref[slot], tl_ref[slot]
            mine_ref[k:, at] = fold3(mxu(ps_ref[...], dh, NT) + mxu(ps_ref[...], dl, NT))
            qb = qs_ref[:, at]
            pd = pd + fold3(mxu(qb, dh) + mxu(qb, dl))
            pt = pt + fold3(mxu(qb, th) + mxu(qb, tl))
    a = mine_ref[k:, :]
    one = pd + pt

    @pl.when(core == 0)
    def _():
        send_ref[:k] = a
        send_ref[k:] = jnp.zeros_like(a)
        mine_ref[:k] = one
        mine_ref[k:] = pt

    @pl.when(core == 1)
    def _():
        send_ref[:k] = one
        send_ref[k:] = pt
        mine_ref[:k] = jnp.zeros_like(a)


def em_step(first, snps_all, core, half, q, keep, got):
    individuals, snps = half.shape
    k = q.shape[0]
    f32, bf16 = jnp.float32, jnp.bfloat16
    return pl.pallas_call(
        functools.partial(em_kernel, first, snps_all),
        out_shape=(
            jax.ShapeDtypeStruct((2 * k, snps), f32),
            jax.ShapeDtypeStruct((2 * k, snps), f32),
            jax.ShapeDtypeStruct((k, individuals), f32),
            jax.ShapeDtypeStruct((k, snps), f32),
        ),
        in_specs=[SMEM] + [VMEM] * 4,
        out_specs=(VMEM,) * 4,
        scratch_shapes=[
            pltpu.VMEM((3 * k, individuals), bf16),
            pltpu.VMEM((individuals, 6 * k), bf16),
            pltpu.VMEM((3 * k, snps), bf16),
            pltpu.VMEM((6 * k, snps), bf16),
        ]
        + [pltpu.VMEM((2, ROWS, snps), bf16)] * 4,
        compiler_params=pltpu.CompilerParams(vmem_limit_bytes=32 * 1024 * 1024),
        cost_estimate=pl.CostEstimate(flops=2 * 20 * k * individuals * snps, bytes_accessed=4 * individuals * snps, transcendentals=individuals * snps),
    )(core, half, q, keep, got)


def swap_cores(x, n_ind):
    return lax.ppermute(x, "ind", [(i, i ^ 1) for i in range(n_ind)])


def exchange(x, mask, n_ind, n_snp):
    n_chip = n_ind // 2
    pairs = []
    for i in range(n_ind):
        for s in range(n_snp):
            if i % 2 == 0 and mask < n_chip:
                pairs.append((i * n_snp + s, (i ^ (2 * mask)) * n_snp + s))
            if i % 2 == 1 and mask < n_snp:
                pairs.append((i * n_snp + s, i * n_snp + (s ^ mask)))
    return lax.ppermute(x, AXES, pairs) if pairs else None


def sum_groups(buf, n_ind, n_snp):
    base = 1
    while base < max(n_ind // 2, n_snp):
        parts = [exchange(buf, m * base, n_ind, n_snp) for m in (1, 2, 3)]
        parts = [part for part in parts if part is not None]
        if len(parts) == 3:
            buf = (buf + parts[2]) + (parts[1] + parts[0])
        else:
            for part in parts:
                buf = buf + part
        base *= 4
    return buf


def place(shard, index, count):
    width = shard.shape[1]
    full = jnp.zeros((shard.shape[0], width * count), shard.dtype)
    return lax.dynamic_update_slice_in_dim(full, shard, index * width, axis=1)


def gather_small(core_id, index, genotypes, ancestry, freqs, n_ind, n_snp):
    k = ancestry.shape[0]
    first_core = core_id[0] == 0
    none = jnp.zeros_like(freqs)
    recv = swap_cores(jnp.where(first_core, ancestry, jnp.concatenate([none, freqs], axis=1)), n_ind)
    zeros = jnp.zeros_like(ancestry)
    mine = jnp.where(first_core, jnp.concatenate([jnp.concatenate([freqs, none], axis=1), zeros]), jnp.concatenate([zeros, ancestry]))
    mine = lax.optimization_barrier(mine)
    own = jnp.concatenate([mine[:k] + recv, mine[k:]])
    own, genotypes = lax.optimization_barrier((own, genotypes))
    half = load_counts(genotypes)
    chunks = [own] + [exchange(own, m, n_ind, n_snp) for m in range(1, n_snp)]
    *chunks, half = lax.optimization_barrier((*chunks, half))
    bit = 1
    while bit < n_snp:
        flip = (index & bit) != 0
        chunks = [jnp.where(flip, chunks[j ^ bit], chunks[j]) for j in range(n_snp)]
        bit *= 2
    full = jnp.concatenate(chunks, axis=1)
    keep = jnp.where(first_core, full[:k], full[k:])
    return half, keep, swap_cores(full[:k], n_ind)


def close_kernel(snps_all, at_ref, q_ref, p_ref, keep_ref, got_ref, q_out, p_out):
    core = at_ref[0]
    keep, got = keep_ref[...], got_ref[...]
    sums = jnp.where(core == 0, keep, got)
    a_sum = jnp.where(core == 0, got, keep)
    k, wide = q_out.shape
    width = p_out.shape[1]
    a_sum = jnp.concatenate([a_sum[:k], a_sum[k:]], axis=1)
    q = q_ref[:, pl.ds(pl.multiple_of(at_ref[1], 128), wide)]
    p = p_ref[:, pl.ds(pl.multiple_of(at_ref[2], 128), width)]
    q_out[...] = new_ancestry(q, a_sum, snps_all)
    up = p * sums[:k]
    p_out[...] = up / (up + (1.0 - p) * sums[k:])


def finish_small(snps_all, core_id, index, at, mine, send, q, p, n_ind, n_snp, shapes):
    k = q.shape[0]
    buf = mine + swap_cores(send, n_ind)
    wide = shapes[0][1]
    half = wide // 2
    chunk = lambda m: lax.dynamic_slice_in_dim(buf, (index ^ m) * wide, wide, axis=1)
    parts = [exchange(chunk(m), m, n_ind, n_snp) for m in range(1, n_snp)]
    total = chunk(0)
    for part in parts[::-1]:
        total = total + part
    first_core = core_id[0] == 0
    fold = lambda x: jnp.concatenate([x[:, :half], x[:, half:]])
    keep = jnp.where(first_core, total[:, :half], fold(total[k:]))
    got = swap_cores(jnp.where(first_core, total[:, half:], fold(total[:k])), n_ind)
    return pl.pallas_call(
        functools.partial(close_kernel, snps_all),
        out_shape=tuple(jax.ShapeDtypeStruct(s, jnp.float32) for s in shapes),
        in_specs=[SMEM] + [VMEM] * 4,
        out_specs=(VMEM, VMEM),
        compiler_params=pltpu.CompilerParams(vmem_limit_bytes=1024 * 1024),
    )(at, q, p, keep, got)


def body(genotypes, ancestry, freqs):
    n_ind, n_snp = lax.axis_size("ind"), lax.axis_size("snp")
    ind, snp = lax.axis_index("ind"), lax.axis_index("snp")
    core = ind % 2
    first_core = core == 0
    index = jnp.where(first_core, ind // 2, snp)
    k = ancestry.shape[0]
    snps_all = genotypes.shape[1] * n_snp
    core_id = core.reshape(1).astype(jnp.int32)
    at = jnp.stack([core, snp * ancestry.shape[1], ind * freqs.shape[1]]).astype(jnp.int32)
    small = n_ind == 2 * n_snp and ancestry.shape[1] == 2 * freqs.shape[1] and freqs.shape[1] % 128 == 0

    if small:
        half, keep, got = gather_small(core_id, index, genotypes, ancestry, freqs, n_ind, n_snp)
        q = keep
    else:
        half = load_counts(genotypes)
        q_at = place(ancestry, snp, n_snp)
        p_at = place(freqs, ind, n_ind)
        q = none = jnp.zeros_like(q_at)
        mine = jnp.concatenate([jnp.where(first_core, p_at, none), jnp.where(first_core, none, q_at)])
        send = jnp.concatenate([jnp.where(first_core, q_at, p_at), none])
        buf = sum_groups(mine + swap_cores(send, n_ind), n_ind, n_snp)
        keep = jnp.where(first_core, buf[:k], buf[k:])
        got = swap_cores(buf[:k], n_ind)
    for step in range(ITERS):
        mine, send, q, p = em_step(step == 0, snps_all, core_id, half, q, keep, got)
        if small and step == ITERS - 1:
            return finish_small(snps_all, core_id, index, at, mine, send, q, p, n_ind, n_snp, (ancestry.shape, freqs.shape))
        buf = sum_groups(mine + swap_cores(send, n_ind), n_ind, n_snp)
        up = p * buf[:k]
        p_new = up / (up + (1.0 - p) * buf[k:])
        keep = jnp.where(first_core, p_new, buf[k:])
        got = swap_cores(jnp.where(first_core, p_new, buf[:k]), n_ind)
    p = jnp.where(first_core, keep, got)
    q = new_ancestry(q, jnp.where(first_core, got, keep), snps_all)
    q_own = lax.dynamic_slice_in_dim(q, snp * ancestry.shape[1], ancestry.shape[1], axis=1)
    p_own = lax.dynamic_slice_in_dim(p, ind * freqs.shape[1], freqs.shape[1], axis=1)
    return (q_own, p_own)


def solution(mesh):
    in_specs = (P("ind", "snp"), P(None, ("ind", "snp")), P(None, ("snp", "ind")))
    out_specs = (P(None, ("ind", "snp")), P(None, ("snp", "ind")))
    return jax.shard_map(body, mesh=mesh, in_specs=in_specs, out_specs=out_specs, check_vma=False)
```

```python
import functools

import jax
import jax.numpy as jnp
from jax import lax
from jax.experimental import pallas as pl
from jax.experimental.pallas import tpu as pltpu
from jax.sharding import PartitionSpec as P

ITERS = 4
AXES = ("ind", "snp")
ROWS = 256
COLS = 256
NT = (((1,), (1,)), ((), ()))
VMEM = pl.BlockSpec(memory_space=pltpu.VMEM)
HBM = pl.BlockSpec(memory_space=pltpu.HBM)


def split3(x):
    one = x.astype(jnp.bfloat16)
    rest = x - one.astype(jnp.float32)
    two = rest.astype(jnp.bfloat16)
    three = (rest - two.astype(jnp.float32)).astype(jnp.bfloat16)
    return one, two, three


def split2(x):
    one = x.astype(jnp.bfloat16)
    return one, (x - one.astype(jnp.float32)).astype(jnp.bfloat16)


def fold3(x):
    k = x.shape[0] // 3
    return x[:k] + x[k : 2 * k] + x[2 * k :]


def mxu(a, b, dims=(((1,), (0,)), ((), ()))):
    return lax.dot_general(a, b, dims, preferred_element_type=jnp.float32)


def new_ancestry(q, a_sum, snps_all):
    rest = snps_all - jnp.sum(q * a_sum, axis=0, keepdims=True)
    return q * (a_sum + rest) * (1.0 / snps_all)


def load_kernel(g_hbm, half_ref, buf, sems):
    n = buf.shape[0]
    rows = buf.shape[1]
    copies = [pltpu.make_async_copy(g_hbm.at[pl.ds(b * rows, rows)], buf.at[b], sems.at[b]) for b in range(n)]
    for copy in copies:
        copy.start()
    for b in range(n):
        copies[b].wait()
        half_ref[pl.ds(b * rows, rows), :] = 0.5 * buf[b].astype(jnp.float32)


def load_counts(genotypes):
    individuals, snps = genotypes.shape
    rows = 128
    n = individuals // rows
    return pl.pallas_call(
        load_kernel,
        out_shape=jax.ShapeDtypeStruct((individuals, snps), jnp.float32),
        in_specs=[HBM],
        out_specs=VMEM,
        scratch_shapes=[pltpu.VMEM((n, rows, snps), jnp.int32), pltpu.SemaphoreType.DMA((n,))],
        compiler_params=pltpu.CompilerParams(vmem_limit_bytes=16 * 1024 * 1024),
        cost_estimate=pl.CostEstimate(flops=individuals * snps, bytes_accessed=4 * individuals * snps, transcendentals=0),
    )(genotypes)


def em_kernel(first, snps_all, g_ref, q_ref, keep_ref, got_ref, mine_ref, send_ref, q_out, p_out, qs_ref, ql_ref, ps_ref, pr_ref, dh_ref, dl_ref, th_ref, tl_ref):
    core = lax.rem(lax.axis_index("ind"), 2)
    keep, got = keep_ref[...], got_ref[...]
    p = jnp.where(core == 0, keep, got)
    a_sum = jnp.where(core == 0, got, keep)
    q = a_sum if first else new_ancestry(q_ref[...], a_sum, snps_all)
    q_out[...] = q
    p_out[...] = p
    k = q.shape[0]
    individuals, snps = g_ref.shape
    q1, q2, q3 = split3(q)
    p1, p2, p3 = split3(p)
    qs_ref[...] = jnp.concatenate([q1, q2, q3], axis=0)
    ps_ref[...] = jnp.concatenate([p1, p2, p3], axis=0)
    ql_ref[...] = jnp.concatenate([q1, q2, q1, q2, q3, q1], axis=0).T
    pr_ref[...] = jnp.concatenate([p1, p1, p2, p2, p1, p3], axis=0)

    def ratios(t):
        at = slice(t // across * ROWS, (t // across + 1) * ROWS)
        to = slice(t % across * COLS, (t % across + 1) * COLS)
        slot = t % 2
        e = mxu(ql_ref[at, :], pr_ref[:, to])
        half = g_ref[at, to]
        d = e * (1.0 - e)
        inv = pltpu.reciprocal(d, approx=True)
        inv = inv * (2.0 - d * inv)
        diff = (half - e) * inv
        two = ((1.0 - half) * e) * inv
        dh_ref[slot], dl_ref[slot] = split2(diff)
        th_ref[slot], tl_ref[slot] = split2(two)

    across = snps // COLS
    tiles = individuals // ROWS * across
    pd = [0.0] * across
    pt = [0.0] * across
    for t in range(tiles + 1):
        if t < tiles:
            ratios(t)
        if t > 0:
            b, c = divmod(t - 1, across)
            slot = (t - 1) % 2
            at = slice(b * ROWS, (b + 1) * ROWS)
            to = slice(c * COLS, (c + 1) * COLS)
            dh, dl, th, tl = dh_ref[slot], dl_ref[slot], th_ref[slot], tl_ref[slot]
            ps = ps_ref[:, to]
            part = fold3(mxu(ps, dh, NT)) + mxu(ps[:k], dl, NT)
            a = part if c == 0 else a + part
            if c == across - 1:
                mine_ref[k:, at] = a
            qb = qs_ref[:, at]
            pd[c] = pd[c] + (fold3(mxu(qb, dh)) + mxu(qb[:k], dl))
            pt[c] = pt[c] + (fold3(mxu(qb, th)) + mxu(qb[:k], tl))
    pd = jnp.concatenate(pd, axis=1)
    pt = jnp.concatenate(pt, axis=1)
    a = mine_ref[k:, :]
    one = pd + pt

    @pl.when(core == 0)
    def _():
        send_ref[:k] = a
        send_ref[k:] = jnp.zeros_like(a)
        mine_ref[:k] = one
        mine_ref[k:] = pt

    @pl.when(core == 1)
    def _():
        send_ref[:k] = one
        send_ref[k:] = pt
        mine_ref[:k] = jnp.zeros_like(a)


def em_step(first, snps_all, half, q, keep, got):
    individuals, snps = half.shape
    k = q.shape[0]
    f32, bf16 = jnp.float32, jnp.bfloat16
    return pl.pallas_call(
        functools.partial(em_kernel, first, snps_all),
        out_shape=(
            jax.ShapeDtypeStruct((2 * k, snps), f32),
            jax.ShapeDtypeStruct((2 * k, snps), f32),
            jax.ShapeDtypeStruct((k, individuals), f32),
            jax.ShapeDtypeStruct((k, snps), f32),
        ),
        in_specs=[VMEM] * 4,
        out_specs=(VMEM,) * 4,
        scratch_shapes=[
            pltpu.VMEM((3 * k, individuals), bf16),
            pltpu.VMEM((individuals, 6 * k), bf16),
            pltpu.VMEM((3 * k, snps), bf16),
            pltpu.VMEM((6 * k, snps), bf16),
        ]
        + [pltpu.VMEM((2, ROWS, COLS), bf16)] * 4,
        compiler_params=pltpu.CompilerParams(vmem_limit_bytes=32 * 1024 * 1024),
        cost_estimate=pl.CostEstimate(flops=2 * 20 * k * individuals * snps, bytes_accessed=4 * individuals * snps, transcendentals=individuals * snps),
    )(half, q, keep, got)


def swap_cores(x, n_ind):
    return lax.ppermute(x, "ind", [(i, i ^ 1) for i in range(n_ind)])


def exchange(x, mask, n_ind, n_snp):
    n_chip = n_ind // 2
    pairs = []
    for i in range(n_ind):
        for s in range(n_snp):
            if i % 2 == 0 and mask < n_chip:
                pairs.append((i * n_snp + s, (i ^ (2 * mask)) * n_snp + s))
            if i % 2 == 1 and mask < n_snp:
                pairs.append((i * n_snp + s, i * n_snp + (s ^ mask)))
    return lax.ppermute(x, AXES, pairs) if pairs else None


def sum_groups(buf, n_ind, n_snp):
    base = 1
    while base < max(n_ind // 2, n_snp):
        parts = [exchange(buf, m * base, n_ind, n_snp) for m in (1, 2, 3)]
        parts = [part for part in parts if part is not None]
        if len(parts) == 3:
            buf = (buf + parts[2]) + (parts[1] + parts[0])
        else:
            for part in parts:
                buf = buf + part
        base *= 4
    return buf


def place(shard, index, count):
    width = shard.shape[1]
    full = jnp.zeros((shard.shape[0], width * count), shard.dtype)
    return lax.dynamic_update_slice_in_dim(full, shard, index * width, axis=1)


def gather_small(first_core, index, genotypes, ancestry, freqs, n_ind, n_snp):
    k = ancestry.shape[0]
    none = jnp.zeros_like(freqs)
    recv = swap_cores(jnp.where(first_core, ancestry, jnp.concatenate([none, freqs], axis=1)), n_ind)
    zeros = jnp.zeros_like(ancestry)
    mine = jnp.where(first_core, jnp.concatenate([jnp.concatenate([freqs, none], axis=1), zeros]), jnp.concatenate([zeros, ancestry]))
    mine = lax.optimization_barrier(mine)
    own = jnp.concatenate([mine[:k] + recv, mine[k:]])
    own, genotypes = lax.optimization_barrier((own, genotypes))
    half = load_counts(genotypes)
    chunks = [own] + [exchange(own, m, n_ind, n_snp) for m in range(1, n_snp)]
    *chunks, half = lax.optimization_barrier((*chunks, half))
    bit = 1
    while bit < n_snp:
        flip = (index & bit) != 0
        chunks = [jnp.where(flip, chunks[j ^ bit], chunks[j]) for j in range(n_snp)]
        bit *= 2
    full = jnp.concatenate(chunks, axis=1)
    keep = jnp.where(first_core, full[:k], full[k:])
    return half, keep, swap_cores(full[:k], n_ind)


def close_kernel(snps_all, q_ref, p_ref, keep_ref, got_ref, q_out, p_out):
    ind = lax.axis_index("ind")
    core = lax.rem(ind, 2)
    keep, got = keep_ref[...], got_ref[...]
    sums = jnp.where(core == 0, keep, got)
    a_sum = jnp.where(core == 0, got, keep)
    k, wide = q_out.shape
    width = p_out.shape[1]
    a_sum = jnp.concatenate([a_sum[:k], a_sum[k:]], axis=1)
    q = q_ref[:, pl.ds(pl.multiple_of(lax.axis_index("snp") * wide, 128), wide)]
    p = p_ref[:, pl.ds(pl.multiple_of(ind * width, 128), width)]
    q_out[...] = new_ancestry(q, a_sum, snps_all)
    up = p * sums[:k]
    p_out[...] = up / (up + (1.0 - p) * sums[k:])


def finish_small(snps_all, first_core, index, mine, send, q, p, n_ind, n_snp, shapes):
    k = q.shape[0]
    buf = mine + swap_cores(send, n_ind)
    wide = shapes[0][1]
    half = wide // 2
    chunk = lambda m: lax.dynamic_slice_in_dim(buf, (index ^ m) * wide, wide, axis=1)
    parts = [exchange(chunk(m), m, n_ind, n_snp) for m in range(1, n_snp)]
    total = chunk(0)
    for part in parts[::-1]:
        total = total + part
    fold = lambda x: jnp.concatenate([x[:, :half], x[:, half:]])
    keep = jnp.where(first_core, total[:, :half], fold(total[k:]))
    got = swap_cores(jnp.where(first_core, total[:, half:], fold(total[:k])), n_ind)
    return pl.pallas_call(
        functools.partial(close_kernel, snps_all),
        out_shape=tuple(jax.ShapeDtypeStruct(s, jnp.float32) for s in shapes),
        in_specs=[VMEM] * 4,
        out_specs=(VMEM, VMEM),
        compiler_params=pltpu.CompilerParams(vmem_limit_bytes=1024 * 1024),
    )(q, p, keep, got)


def body(genotypes, ancestry, freqs):
    n_ind, n_snp = lax.axis_size("ind"), lax.axis_size("snp")
    ind, snp = lax.axis_index("ind"), lax.axis_index("snp")
    core = ind % 2
    first_core = core == 0
    index = jnp.where(first_core, ind // 2, snp)
    k = ancestry.shape[0]
    snps_all = genotypes.shape[1] * n_snp
    small = n_ind == 2 * n_snp and ancestry.shape[1] == 2 * freqs.shape[1] and freqs.shape[1] % 128 == 0

    if small:
        half, keep, got = gather_small(first_core, index, genotypes, ancestry, freqs, n_ind, n_snp)
        q = keep
    else:
        half = load_counts(genotypes)
        q_at = place(ancestry, snp, n_snp)
        p_at = place(freqs, ind, n_ind)
        q = none = jnp.zeros_like(q_at)
        mine = jnp.concatenate([jnp.where(first_core, p_at, none), jnp.where(first_core, none, q_at)])
        send = jnp.concatenate([jnp.where(first_core, q_at, p_at), none])
        buf = sum_groups(mine + swap_cores(send, n_ind), n_ind, n_snp)
        keep = jnp.where(first_core, buf[:k], buf[k:])
        got = swap_cores(buf[:k], n_ind)
    for step in range(ITERS):
        mine, send, q, p = em_step(step == 0, snps_all, half, q, keep, got)
        if small and step == ITERS - 1:
            return finish_small(snps_all, first_core, index, mine, send, q, p, n_ind, n_snp, (ancestry.shape, freqs.shape))
        buf = sum_groups(mine + swap_cores(send, n_ind), n_ind, n_snp)
        up = p * buf[:k]
        p_new = up / (up + (1.0 - p) * buf[k:])
        keep = jnp.where(first_core, p_new, buf[k:])
        got = swap_cores(jnp.where(first_core, p_new, buf[:k]), n_ind)
    p = jnp.where(first_core, keep, got)
    q = new_ancestry(q, jnp.where(first_core, got, keep), snps_all)
    q_own = lax.dynamic_slice_in_dim(q, snp * ancestry.shape[1], ancestry.shape[1], axis=1)
    p_own = lax.dynamic_slice_in_dim(p, ind * freqs.shape[1], freqs.shape[1], axis=1)
    return (q_own, p_own)


def solution(mesh):
    in_specs = (P("ind", "snp"), P(None, ("ind", "snp")), P(None, ("snp", "ind")))
    out_specs = (P(None, ("ind", "snp")), P(None, ("snp", "ind")))
    return jax.shard_map(body, mesh=mesh, in_specs=in_specs, out_specs=out_specs, check_vma=False)
```

```python
import functools

import jax
import jax.numpy as jnp
from jax import lax
from jax.experimental import pallas as pl
from jax.experimental.pallas import tpu as pltpu
from jax.sharding import PartitionSpec as P

ITERS = 4
AXES = ("ind", "snp")
ROWS = 256
COLS = 256
NT = (((1,), (1,)), ((), ()))
VMEM = pl.BlockSpec(memory_space=pltpu.VMEM)
HBM = pl.BlockSpec(memory_space=pltpu.HBM)


def split3(x):
    one = x.astype(jnp.bfloat16)
    rest = x - one.astype(jnp.float32)
    two = rest.astype(jnp.bfloat16)
    three = (rest - two.astype(jnp.float32)).astype(jnp.bfloat16)
    return one, two, three


def split2(x):
    one = x.astype(jnp.bfloat16)
    return one, (x - one.astype(jnp.float32)).astype(jnp.bfloat16)


def fold3(x):
    k = x.shape[0] // 3
    return x[:k] + x[k : 2 * k] + x[2 * k :]


def mxu(a, b, dims=(((1,), (0,)), ((), ()))):
    return lax.dot_general(a, b, dims, preferred_element_type=jnp.float32)


def new_ancestry(q, a_sum, snps_all):
    rest = snps_all - jnp.sum(q * a_sum, axis=0, keepdims=True)
    return q * (a_sum + rest) * (1.0 / snps_all)


def load_kernel(g_hbm, half_ref, buf, sems):
    n = buf.shape[0]
    rows = buf.shape[1]
    copies = [pltpu.make_async_copy(g_hbm.at[pl.ds(b * rows, rows)], buf.at[b], sems.at[b]) for b in range(n)]
    for copy in copies:
        copy.start()
    for b in range(n):
        copies[b].wait()
        half_ref[pl.ds(b * rows, rows), :] = 0.5 * buf[b].astype(jnp.float32)


def load_counts(genotypes):
    individuals, snps = genotypes.shape
    rows = 128
    n = individuals // rows
    return pl.pallas_call(
        load_kernel,
        out_shape=jax.ShapeDtypeStruct((individuals, snps), jnp.float32),
        in_specs=[HBM],
        out_specs=VMEM,
        scratch_shapes=[pltpu.VMEM((n, rows, snps), jnp.int32), pltpu.SemaphoreType.DMA((n,))],
        compiler_params=pltpu.CompilerParams(vmem_limit_bytes=46 * 1024 * 1024),
        cost_estimate=pl.CostEstimate(flops=individuals * snps, bytes_accessed=4 * individuals * snps, transcendentals=0),
    )(genotypes)


def em_kernel(first, snps_all, g_ref, q_ref, keep_ref, got_ref, mine_ref, send_ref, q_out, p_out, qs_ref, ql_ref, ps_ref, pr_ref, dh_ref, dl_ref, th_ref, tl_ref):
    core = lax.rem(lax.axis_index("ind"), 2)
    keep, got = keep_ref[...], got_ref[...]
    p = jnp.where(core == 0, keep, got)
    a_sum = jnp.where(core == 0, got, keep)
    q = a_sum if first else new_ancestry(q_ref[...], a_sum, snps_all)
    q_out[...] = q
    p_out[...] = p
    k = q.shape[0]
    individuals, snps = g_ref.shape
    q1, q2, q3 = split3(q)
    p1, p2, p3 = split3(p)
    qs_ref[...] = jnp.concatenate([q1, q2, q3], axis=0)
    ps_ref[...] = jnp.concatenate([p1, p2, p3], axis=0)
    ql_ref[...] = jnp.concatenate([q1, q2, q1, q2, q3, q1], axis=0).T
    pr_ref[...] = jnp.concatenate([p1, p1, p2, p2, p1, p3], axis=0)

    def ratios(t):
        at = slice(t // across * ROWS, (t // across + 1) * ROWS)
        to = slice(t % across * COLS, (t % across + 1) * COLS)
        slot = t % 2
        e = mxu(ql_ref[at, :], pr_ref[:, to])
        half = g_ref[at, to]
        two = (1.0 - half) * pltpu.reciprocal(1.0 - e)
        diff = half * pltpu.reciprocal(e) - two
        dh_ref[slot], dl_ref[slot] = split2(diff)
        th_ref[slot], tl_ref[slot] = split2(two)

    across = snps // COLS
    tiles = individuals // ROWS * across
    pd = [0.0] * across
    pt = [0.0] * across
    for t in range(tiles + 1):
        if t < tiles:
            ratios(t)
        if t > 0:
            b, c = divmod(t - 1, across)
            slot = (t - 1) % 2
            at = slice(b * ROWS, (b + 1) * ROWS)
            to = slice(c * COLS, (c + 1) * COLS)
            dh, dl, th, tl = dh_ref[slot], dl_ref[slot], th_ref[slot], tl_ref[slot]
            ps = ps_ref[:, to]
            part = fold3(mxu(ps, dh, NT)) + mxu(ps[:k], dl, NT)
            a = part if c == 0 else a + part
            if c == across - 1:
                mine_ref[k:, at] = a
            qb = qs_ref[:, at]
            pd[c] = pd[c] + (fold3(mxu(qb, dh)) + mxu(qb[:k], dl))
            pt[c] = pt[c] + (fold3(mxu(qb, th)) + mxu(qb[:k], tl))
    pd = jnp.concatenate(pd, axis=1)
    pt = jnp.concatenate(pt, axis=1)
    a = mine_ref[k:, :]
    one = pd + pt

    @pl.when(core == 0)
    def _():
        send_ref[:k] = a
        send_ref[k:] = jnp.zeros_like(a)
        mine_ref[:k] = one
        mine_ref[k:] = pt

    @pl.when(core == 1)
    def _():
        send_ref[:k] = one
        send_ref[k:] = pt
        mine_ref[:k] = jnp.zeros_like(a)


def em_step(first, snps_all, half, q, keep, got):
    individuals, snps = half.shape
    k = q.shape[0]
    f32, bf16 = jnp.float32, jnp.bfloat16
    return pl.pallas_call(
        functools.partial(em_kernel, first, snps_all),
        out_shape=(
            jax.ShapeDtypeStruct((2 * k, snps), f32),
            jax.ShapeDtypeStruct((2 * k, snps), f32),
            jax.ShapeDtypeStruct((k, individuals), f32),
            jax.ShapeDtypeStruct((k, snps), f32),
        ),
        in_specs=[VMEM] * 4,
        out_specs=(VMEM,) * 4,
        scratch_shapes=[
            pltpu.VMEM((3 * k, individuals), bf16),
            pltpu.VMEM((individuals, 6 * k), bf16),
            pltpu.VMEM((3 * k, snps), bf16),
            pltpu.VMEM((6 * k, snps), bf16),
        ]
        + [pltpu.VMEM((2, ROWS, COLS), bf16)] * 4,
        compiler_params=pltpu.CompilerParams(vmem_limit_bytes=32 * 1024 * 1024),
        cost_estimate=pl.CostEstimate(flops=2 * 20 * k * individuals * snps, bytes_accessed=4 * individuals * snps, transcendentals=individuals * snps),
    )(half, q, keep, got)


def swap_cores(x, n_ind):
    return lax.ppermute(x, "ind", [(i, i ^ 1) for i in range(n_ind)])


def exchange(x, mask, n_ind, n_snp):
    n_chip = n_ind // 2
    pairs = []
    for i in range(n_ind):
        for s in range(n_snp):
            if i % 2 == 0 and mask < n_chip:
                pairs.append((i * n_snp + s, (i ^ (2 * mask)) * n_snp + s))
            if i % 2 == 1 and mask < n_snp:
                pairs.append((i * n_snp + s, i * n_snp + (s ^ mask)))
    return lax.ppermute(x, AXES, pairs) if pairs else None


def sum_groups(buf, n_ind, n_snp):
    base = 1
    while base < max(n_ind // 2, n_snp):
        parts = [exchange(buf, m * base, n_ind, n_snp) for m in (2, 1, 3)]
        parts = [part for part in parts if part is not None]
        if len(parts) == 3:
            buf = (buf + parts[2]) + (parts[1] + parts[0])
        else:
            for part in parts:
                buf = buf + part
        base *= 4
    return buf


def place(shard, index, count):
    width = shard.shape[1]
    full = jnp.zeros((shard.shape[0], width * count), shard.dtype)
    return lax.dynamic_update_slice_in_dim(full, shard, index * width, axis=1)


def gather_small(first_core, index, genotypes, ancestry, freqs, n_ind, n_snp):
    k = ancestry.shape[0]
    none = jnp.zeros_like(freqs)
    recv = swap_cores(jnp.where(first_core, ancestry, jnp.concatenate([none, freqs], axis=1)), n_ind)
    zeros = jnp.zeros_like(ancestry)
    mine = jnp.where(first_core, jnp.concatenate([jnp.concatenate([freqs, none], axis=1), zeros]), jnp.concatenate([zeros, ancestry]))
    mine = lax.optimization_barrier(mine)
    own = jnp.concatenate([mine[:k] + recv, mine[k:]])
    own, genotypes = lax.optimization_barrier((own, genotypes))
    half = load_counts(genotypes)
    chunks = [own] + [exchange(own, m, n_ind, n_snp) for m in range(1, n_snp)]
    *chunks, half = lax.optimization_barrier((*chunks, half))
    bit = 1
    while bit < n_snp:
        flip = (index & bit) != 0
        chunks = [jnp.where(flip, chunks[j ^ bit], chunks[j]) for j in range(n_snp)]
        bit *= 2
    full = jnp.concatenate(chunks, axis=1)
    keep = jnp.where(first_core, full[:k], full[k:])
    return half, keep, swap_cores(full[:k], n_ind)


def close_kernel(snps_all, q_ref, p_ref, keep_ref, got_ref, q_out, p_out):
    ind = lax.axis_index("ind")
    core = lax.rem(ind, 2)
    keep, got = keep_ref[...], got_ref[...]
    sums = jnp.where(core == 0, keep, got)
    a_sum = jnp.where(core == 0, got, keep)
    k, wide = q_out.shape
    width = p_out.shape[1]
    a_sum = jnp.concatenate([a_sum[:k], a_sum[k:]], axis=1)
    q = q_ref[:, pl.ds(pl.multiple_of(lax.axis_index("snp") * wide, 128), wide)]
    p = p_ref[:, pl.ds(pl.multiple_of(ind * width, 128), width)]
    q_out[...] = new_ancestry(q, a_sum, snps_all)
    up = p * sums[:k]
    p_out[...] = up / (up + (1.0 - p) * sums[k:])


def finish_small(snps_all, first_core, index, mine, send, q, p, n_ind, n_snp, shapes):
    k = q.shape[0]
    buf = mine + swap_cores(send, n_ind)
    wide = shapes[0][1]
    half = wide // 2
    chunk = lambda m: lax.dynamic_slice_in_dim(buf, (index ^ m) * wide, wide, axis=1)
    parts = [exchange(chunk(m), m, n_ind, n_snp) for m in range(1, n_snp)]
    total = chunk(0)
    for part in parts[::-1]:
        total = total + part
    fold = lambda x: jnp.concatenate([x[:, :half], x[:, half:]])
    keep = jnp.where(first_core, total[:, :half], fold(total[k:]))
    got = swap_cores(jnp.where(first_core, total[:, half:], fold(total[:k])), n_ind)
    return pl.pallas_call(
        functools.partial(close_kernel, snps_all),
        out_shape=tuple(jax.ShapeDtypeStruct(s, jnp.float32) for s in shapes),
        in_specs=[VMEM] * 4,
        out_specs=(VMEM, VMEM),
        compiler_params=pltpu.CompilerParams(vmem_limit_bytes=1024 * 1024),
    )(q, p, keep, got)


def body(genotypes, ancestry, freqs):
    n_ind, n_snp = lax.axis_size("ind"), lax.axis_size("snp")
    ind, snp = lax.axis_index("ind"), lax.axis_index("snp")
    core = ind % 2
    first_core = core == 0
    index = jnp.where(first_core, ind // 2, snp)
    k = ancestry.shape[0]
    snps_all = genotypes.shape[1] * n_snp
    small = n_ind == 2 * n_snp and ancestry.shape[1] == 2 * freqs.shape[1] and freqs.shape[1] % 128 == 0

    if small:
        half, keep, got = gather_small(first_core, index, genotypes, ancestry, freqs, n_ind, n_snp)
        q = keep
    else:
        half = load_counts(genotypes)
        q_at = place(ancestry, snp, n_snp)
        p_at = place(freqs, ind, n_ind)
        q = none = jnp.zeros_like(q_at)
        mine = jnp.concatenate([jnp.where(first_core, p_at, none), jnp.where(first_core, none, q_at)])
        send = jnp.concatenate([jnp.where(first_core, q_at, p_at), none])
        buf = sum_groups(mine + swap_cores(send, n_ind), n_ind, n_snp)
        keep = jnp.where(first_core, buf[:k], buf[k:])
        got = swap_cores(buf[:k], n_ind)
    for step in range(ITERS):
        mine, send, q, p = em_step(step == 0, snps_all, half, q, keep, got)
        if small and step == ITERS - 1:
            return finish_small(snps_all, first_core, index, mine, send, q, p, n_ind, n_snp, (ancestry.shape, freqs.shape))
        buf = sum_groups(mine + swap_cores(send, n_ind), n_ind, n_snp)
        up = p * buf[:k]
        p_new = up / (up + (1.0 - p) * buf[k:])
        keep = jnp.where(first_core, p_new, buf[k:])
        got = swap_cores(jnp.where(first_core, p_new, buf[:k]), n_ind)
    p = jnp.where(first_core, keep, got)
    q = new_ancestry(q, jnp.where(first_core, got, keep), snps_all)
    q_own = lax.dynamic_slice_in_dim(q, snp * ancestry.shape[1], ancestry.shape[1], axis=1)
    p_own = lax.dynamic_slice_in_dim(p, ind * freqs.shape[1], freqs.shape[1], axis=1)
    return (q_own, p_own)


def solution(mesh):
    in_specs = (P("ind", "snp"), P(None, ("ind", "snp")), P(None, ("snp", "ind")))
    out_specs = (P(None, ("ind", "snp")), P(None, ("snp", "ind")))
    return jax.shard_map(body, mesh=mesh, in_specs=in_specs, out_specs=out_specs, check_vma=False)
```

```python
import functools

import jax
import jax.numpy as jnp
from jax import lax
from jax.experimental import pallas as pl
from jax.experimental.pallas import tpu as pltpu
from jax.sharding import PartitionSpec as P

ITERS = 4
AXES = ("ind", "snp")
ROWS = 256
COLS = 256
NT = (((1,), (1,)), ((), ()))
VMEM = pl.BlockSpec(memory_space=pltpu.VMEM)
HBM = pl.BlockSpec(memory_space=pltpu.HBM)


def split3(x):
    one = x.astype(jnp.bfloat16)
    rest = x - one.astype(jnp.float32)
    two = rest.astype(jnp.bfloat16)
    three = (rest - two.astype(jnp.float32)).astype(jnp.bfloat16)
    return one, two, three


def split2(x):
    one = x.astype(jnp.bfloat16)
    return one, (x - one.astype(jnp.float32)).astype(jnp.bfloat16)


def fold3(x):
    k = x.shape[0] // 3
    return x[:k] + x[k : 2 * k] + x[2 * k :]


def mxu(a, b, dims=(((1,), (0,)), ((), ()))):
    return lax.dot_general(a, b, dims, preferred_element_type=jnp.float32)


def new_ancestry(q, a_sum, snps_all):
    rest = snps_all - jnp.sum(q * a_sum, axis=0, keepdims=True)
    return q * (a_sum + rest) * (1.0 / snps_all)


def load_kernel(g_hbm, half_ref, buf, sems):
    n = buf.shape[0]
    rows = buf.shape[1]
    copies = [pltpu.make_async_copy(g_hbm.at[pl.ds(b * rows, rows)], buf.at[b], sems.at[b]) for b in range(n)]
    for copy in copies:
        copy.start()
    for b in range(n):
        copies[b].wait()
        half_ref[pl.ds(b * rows, rows), :] = 0.5 * buf[b].astype(jnp.float32)


def load_counts(genotypes):
    individuals, snps = genotypes.shape
    rows = 128
    n = individuals // rows
    return pl.pallas_call(
        load_kernel,
        out_shape=jax.ShapeDtypeStruct((individuals, snps), jnp.float32),
        in_specs=[HBM],
        out_specs=VMEM,
        scratch_shapes=[pltpu.VMEM((n, rows, snps), jnp.int32), pltpu.SemaphoreType.DMA((n,))],
        compiler_params=pltpu.CompilerParams(vmem_limit_bytes=46 * 1024 * 1024),
        cost_estimate=pl.CostEstimate(flops=individuals * snps, bytes_accessed=4 * individuals * snps, transcendentals=0),
    )(genotypes)


def em_kernel(first, snps_all, g_ref, q_ref, keep_ref, got_ref, mine_ref, send_ref, q_out, p_out, qs_ref, ql_ref, ps_ref, pr_ref, dh_ref, dl_ref, th_ref, tl_ref):
    core = lax.rem(lax.axis_index("ind"), 2)
    keep, got = keep_ref[...], got_ref[...]
    p = jnp.where(core == 0, keep, got)
    a_sum = jnp.where(core == 0, got, keep)
    q = a_sum if first else new_ancestry(q_ref[...], a_sum, snps_all)
    q_out[...] = q
    p_out[...] = p
    k = q.shape[0]
    individuals, snps = g_ref.shape
    q1, q2, q3 = split3(q)
    p1, p2, p3 = split3(p)
    qs_ref[...] = jnp.concatenate([q1, q2, q3], axis=0)
    ps_ref[...] = jnp.concatenate([p1, p2, p3], axis=0)
    ql_ref[...] = jnp.concatenate([q1, q2, q1, q2, q3, q1], axis=0).T
    pr_ref[...] = jnp.concatenate([p1, p1, p2, p2, p1, p3], axis=0)

    def ratios(t):
        at = slice(t // across * ROWS, (t // across + 1) * ROWS)
        to = slice(t % across * COLS, (t % across + 1) * COLS)
        slot = t % 2
        e = mxu(ql_ref[at, :], pr_ref[:, to])
        half = g_ref[at, to]
        two = (1.0 - half) * pltpu.reciprocal(1.0 - e)
        diff = half * pltpu.reciprocal(e) - two
        dh_ref[slot], dl_ref[slot] = split2(diff)
        th_ref[slot], tl_ref[slot] = split2(two)

    across = snps // COLS
    tiles = individuals // ROWS * across
    pd = [0.0] * across
    pt = [0.0] * across
    for t in range(tiles + 1):
        if t < tiles:
            ratios(t)
        if t > 0:
            b, c = divmod(t - 1, across)
            slot = (t - 1) % 2
            at = slice(b * ROWS, (b + 1) * ROWS)
            to = slice(c * COLS, (c + 1) * COLS)
            dh, dl, th, tl = dh_ref[slot], dl_ref[slot], th_ref[slot], tl_ref[slot]
            ps = ps_ref[:, to]
            part = fold3(mxu(ps, dh, NT)) + mxu(ps[:k], dl, NT)
            a = part if c == 0 else a + part
            if c == across - 1:
                mine_ref[k:, at] = a
            qb = qs_ref[:, at]
            pd[c] = pd[c] + (fold3(mxu(qb, dh)) + mxu(qb[:k], dl))
            pt[c] = pt[c] + (fold3(mxu(qb, th)) + mxu(qb[:k], tl))
    pd = jnp.concatenate(pd, axis=1)
    pt = jnp.concatenate(pt, axis=1)
    a = mine_ref[k:, :]
    one = pd + pt

    @pl.when(core == 0)
    def _():
        send_ref[:k] = a
        send_ref[k:] = jnp.zeros_like(a)
        mine_ref[:k] = one
        mine_ref[k:] = pt

    @pl.when(core == 1)
    def _():
        send_ref[:k] = one
        send_ref[k:] = pt
        mine_ref[:k] = jnp.zeros_like(a)


def em_step(first, snps_all, half, q, keep, got):
    individuals, snps = half.shape
    k = q.shape[0]
    f32, bf16 = jnp.float32, jnp.bfloat16
    return pl.pallas_call(
        functools.partial(em_kernel, first, snps_all),
        out_shape=(
            jax.ShapeDtypeStruct((2 * k, snps), f32),
            jax.ShapeDtypeStruct((2 * k, snps), f32),
            jax.ShapeDtypeStruct((k, individuals), f32),
            jax.ShapeDtypeStruct((k, snps), f32),
        ),
        in_specs=[VMEM] * 4,
        out_specs=(VMEM,) * 4,
        scratch_shapes=[
            pltpu.VMEM((3 * k, individuals), bf16),
            pltpu.VMEM((individuals, 6 * k), bf16),
            pltpu.VMEM((3 * k, snps), bf16),
            pltpu.VMEM((6 * k, snps), bf16),
        ]
        + [pltpu.VMEM((2, ROWS, COLS), bf16)] * 4,
        compiler_params=pltpu.CompilerParams(vmem_limit_bytes=32 * 1024 * 1024),
        cost_estimate=pl.CostEstimate(flops=2 * 20 * k * individuals * snps, bytes_accessed=4 * individuals * snps, transcendentals=individuals * snps),
    )(half, q, keep, got)


def swap_cores(x, n_ind):
    return lax.ppermute(x, "ind", [(i, i ^ 1) for i in range(n_ind)])


def exchange(x, mask, n_ind, n_snp):
    n_chip = n_ind // 2
    pairs = []
    for i in range(n_ind):
        for s in range(n_snp):
            if i % 2 == 0 and mask < n_chip:
                pairs.append((i * n_snp + s, (i ^ (2 * mask)) * n_snp + s))
            if i % 2 == 1 and mask < n_snp:
                pairs.append((i * n_snp + s, i * n_snp + (s ^ mask)))
    return lax.ppermute(x, AXES, pairs) if pairs else None


def sum_groups(buf, n_ind, n_snp):
    base = 1
    while base < max(n_ind // 2, n_snp):
        parts = [exchange(buf, m * base, n_ind, n_snp) for m in (2, 1, 3)]
        parts = [part for part in parts if part is not None]
        if len(parts) == 3:
            buf = (buf + parts[2]) + (parts[1] + parts[0])
        else:
            for part in parts:
                buf = buf + part
        base *= 4
    return buf


def place(shard, index, count):
    width = shard.shape[1]
    full = jnp.zeros((shard.shape[0], width * count), shard.dtype)
    return lax.dynamic_update_slice_in_dim(full, shard, index * width, axis=1)


def gather_small(first_core, index, genotypes, ancestry, freqs, n_ind, n_snp):
    k = ancestry.shape[0]
    none = jnp.zeros_like(freqs)
    recv = swap_cores(jnp.where(first_core, ancestry, jnp.concatenate([none, freqs], axis=1)), n_ind)
    zeros = jnp.zeros_like(ancestry)
    mine = jnp.where(first_core, jnp.concatenate([jnp.concatenate([freqs, none], axis=1), zeros]), jnp.concatenate([zeros, ancestry]))
    mine = lax.optimization_barrier(mine)
    own = jnp.concatenate([mine[:k] + recv, mine[k:]])
    own, genotypes = lax.optimization_barrier((own, genotypes))
    half = load_counts(genotypes)
    chunks = [own] + [exchange(own, m, n_ind, n_snp) for m in range(1, n_snp)]
    chunks[3], half = lax.optimization_barrier((chunks[3], half))
    bit = 1
    while bit < n_snp:
        flip = (index & bit) != 0
        chunks = [jnp.where(flip, chunks[j ^ bit], chunks[j]) for j in range(n_snp)]
        bit *= 2
    full = jnp.concatenate(chunks, axis=1)
    keep = jnp.where(first_core, full[:k], full[k:])
    return half, keep, swap_cores(full[:k], n_ind)


def close_kernel(snps_all, q_ref, p_ref, keep_ref, got_ref, q_out, p_out):
    ind = lax.axis_index("ind")
    core = lax.rem(ind, 2)
    keep, got = keep_ref[...], got_ref[...]
    sums = jnp.where(core == 0, keep, got)
    a_sum = jnp.where(core == 0, got, keep)
    k, wide = q_out.shape
    width = p_out.shape[1]
    a_sum = jnp.concatenate([a_sum[:k], a_sum[k:]], axis=1)
    q = q_ref[:, pl.ds(pl.multiple_of(lax.axis_index("snp") * wide, 128), wide)]
    p = p_ref[:, pl.ds(pl.multiple_of(ind * width, 128), width)]
    q_out[...] = new_ancestry(q, a_sum, snps_all)
    up = p * sums[:k]
    p_out[...] = up / (up + (1.0 - p) * sums[k:])


def finish_small(snps_all, first_core, index, mine, send, q, p, n_ind, n_snp, shapes):
    k = q.shape[0]
    buf = mine + swap_cores(send, n_ind)
    wide = shapes[0][1]
    half = wide // 2
    chunk = lambda m: lax.dynamic_slice_in_dim(buf, (index ^ m) * wide, wide, axis=1)
    parts = [exchange(chunk(m), m, n_ind, n_snp) for m in range(1, n_snp)]
    total = chunk(0)
    for part in parts[::-1]:
        total = total + part
    fold = lambda x: jnp.concatenate([x[:, :half], x[:, half:]])
    keep = jnp.where(first_core, total[:, :half], fold(total[k:]))
    got = swap_cores(jnp.where(first_core, total[:, half:], fold(total[:k])), n_ind)
    return pl.pallas_call(
        functools.partial(close_kernel, snps_all),
        out_shape=tuple(jax.ShapeDtypeStruct(s, jnp.float32) for s in shapes),
        in_specs=[VMEM] * 4,
        out_specs=(VMEM, VMEM),
        compiler_params=pltpu.CompilerParams(vmem_limit_bytes=1024 * 1024),
    )(q, p, keep, got)


def body(genotypes, ancestry, freqs):
    n_ind, n_snp = lax.axis_size("ind"), lax.axis_size("snp")
    ind, snp = lax.axis_index("ind"), lax.axis_index("snp")
    core = ind % 2
    first_core = core == 0
    index = jnp.where(first_core, ind // 2, snp)
    k = ancestry.shape[0]
    snps_all = genotypes.shape[1] * n_snp
    small = n_ind == 2 * n_snp and ancestry.shape[1] == 2 * freqs.shape[1] and freqs.shape[1] % 128 == 0

    if small:
        half, keep, got = gather_small(first_core, index, genotypes, ancestry, freqs, n_ind, n_snp)
        q = keep
    else:
        half = load_counts(genotypes)
        q_at = place(ancestry, snp, n_snp)
        p_at = place(freqs, ind, n_ind)
        q = none = jnp.zeros_like(q_at)
        mine = jnp.concatenate([jnp.where(first_core, p_at, none), jnp.where(first_core, none, q_at)])
        send = jnp.concatenate([jnp.where(first_core, q_at, p_at), none])
        buf = sum_groups(mine + swap_cores(send, n_ind), n_ind, n_snp)
        keep = jnp.where(first_core, buf[:k], buf[k:])
        got = swap_cores(buf[:k], n_ind)
    for step in range(ITERS):
        mine, send, q, p = em_step(step == 0, snps_all, half, q, keep, got)
        if small and step == ITERS - 1:
            return finish_small(snps_all, first_core, index, mine, send, q, p, n_ind, n_snp, (ancestry.shape, freqs.shape))
        buf = sum_groups(mine + swap_cores(send, n_ind), n_ind, n_snp)
        up = p * buf[:k]
        p_new = up / (up + (1.0 - p) * buf[k:])
        keep = jnp.where(first_core, p_new, buf[k:])
        got = swap_cores(jnp.where(first_core, p_new, buf[:k]), n_ind)
    p = jnp.where(first_core, keep, got)
    q = new_ancestry(q, jnp.where(first_core, got, keep), snps_all)
    q_own = lax.dynamic_slice_in_dim(q, snp * ancestry.shape[1], ancestry.shape[1], axis=1)
    p_own = lax.dynamic_slice_in_dim(p, ind * freqs.shape[1], freqs.shape[1], axis=1)
    return (q_own, p_own)


def solution(mesh):
    in_specs = (P("ind", "snp"), P(None, ("ind", "snp")), P(None, ("snp", "ind")))
    out_specs = (P(None, ("ind", "snp")), P(None, ("snp", "ind")))
    return jax.shard_map(body, mesh=mesh, in_specs=in_specs, out_specs=out_specs, check_vma=False)
```
